128 devices in a mesh: sec: 32 (over z, y, core), mpo: 4 (over x).
Axes of the slice: x: 4, y: 4, z: 4, core: 2. Of those that a mesh axis runs over, the one named last changes fastest.
Arguments:
- psi: bfloat16 [32, 4, 512, 512], P('sec'), may hold values from -6 to 6
- left_env: bfloat16 [16, 32, 4, 512, 512], P('mpo', 'sec'), may hold values from -0.125 to 0.125
- right_env: bfloat16 [16, 32, 4, 512, 512], P('mpo', 'sec'), may hold values from -0.25 to 0.25
- shifts: int32 [16, 2], P('mpo'), may hold values from -1 to 1, as said below
Outputs:
- h_psi: bfloat16 [32, 4, 512, 512], P('sec', 'mpo')
The draws below stay inside these ranges and needn't reach their ends.
Inputs may be any that keep to these rules, and one draw needn't show every extreme that they name: `shifts`: in every term the row shift and the spin shift are both zero or both nonzero; each of the pairs (0, 0), (1, 1), (1, -1), (-1, 1), (-1, -1) occurs.
All inputs are finite; a program needn't handle non-finite values.
Results may differ from the reference program's by a relative error of at most 0.0049.
Values may be sent and summed in bfloat16 or wider, within the bound.
A program may use at most 128 MiB of HBM per device.

```python
import jax
import jax.numpy as jnp
from jax import lax

B = 512
QS = 4
NW = 16
NQ = 32


def draw_shifts(key, part):
    key = jax.random.fold_in(key, 7)
    codes = jax.random.permutation(key, NW) % 5
    table = jnp.array([[0, 0], [1, 1], [1, -1], [-1, 1], [-1, -1]], dtype=jnp.int32)
    return table[codes].astype(jnp.int32)


def block_levels(key, extent, shards, low, top_value):
    loudness = 1.0
    for dim, blocks in shards:
        draws = jax.random.uniform(jax.random.fold_in(jax.random.fold_in(key, 6), dim), (blocks,), jnp.float32, low / len(shards), top_value / len(shards))
        loudness = loudness * jnp.repeat(jnp.exp(draws), extent[dim] // blocks).reshape((-1,) + (1,) * (len(extent) - 1 - dim))
    return loudness


def scatter_about(key, dims, width, bound, shards=(), kind=jnp.bfloat16):
    values = jax.random.normal(key, dims, jnp.float32) * width
    if len(shards) > 0:
        values = block_levels(key, dims, shards, -0.22, 0.18) * values
    return jnp.clip(values, min=-bound, max=bound).astype(kind)


def setup_inputs(seed: int = 0) -> dict:
    streams_of = jax.random.split(jax.random.key(seed), 5)
    psi = scatter_about(streams_of[0], (NQ, QS, B, B), 1.0, 6.0, ((0, 32),))
    left_env = scatter_about(streams_of[1], (NW, NQ, QS, B, B), (B * 4) ** -0.5, 0.125, ((0, 4), (1, 32)))
    right_env = scatter_about(streams_of[2], (NW, NQ, QS, B, B), B ** -0.5, 0.25, ((0, 4), (1, 32)))
    shifts = draw_shifts(jax.random.fold_in(streams_of[4], 71), 0)
    return {"psi": psi, "left_env": left_env, "right_env": right_env, "shifts": shifts}


def reference(psi, left_env, right_env, shifts):
    padded = jnp.pad(psi, ((1, 1), (1, 1), (0, 0), (0, 0)))

    def term(total, index):
        row_shift = shifts[index, 0].astype(jnp.int32)
        col_shift = shifts[index, 1].astype(jnp.int32)
        zero = jnp.int32(0)
        source = lax.dynamic_slice(padded, (jnp.int32(1) - row_shift, jnp.int32(1) - col_shift, zero, zero), (NQ, QS, B, B))
        inner = jnp.einsum("nsab,nsbc->nsac", source.astype(jnp.float32), right_env[index].astype(jnp.float32)).astype(jnp.bfloat16)
        outer = jnp.einsum("nsab,nsbc->nsac", left_env[index].astype(jnp.float32), inner.astype(jnp.float32))
        return total + outer, None

    total, unused = lax.scan(term, jnp.zeros((NQ, QS, B, B), jnp.float32), jnp.arange(NW, dtype=jnp.int32))
    return total.astype(jnp.bfloat16)
```

```python
import functools

import jax
import jax.numpy as jnp
from jax import lax
from jax.experimental import pallas as pl
from jax.experimental.pallas import tpu as pltpu
from jax.sharding import PartitionSpec as P

MESH = pl.DeviceIdType.MESH
f32, bf16 = jnp.float32, jnp.bfloat16
dot = functools.partial(jnp.dot, preferred_element_type=f32)

SECTORS = ((1, 2, 1, 2), (3, 1, 2, 0), (2, 3, 0, 1), (0, 0, 3, 3))
TARGETS = ((0, 3, 0, 3), (2, 0, 3, 1), (3, 2, 1, 0), (1, 1, 2, 2))


def entry(row, x):
    code = sum(value * 4**i for i, value in enumerate(row))
    power = (1 + 3 * lax.rem(x, 2)) * (1 + 15 * (x // 2))
    return lax.rem(code // power, 4)


def kernel(rows, shifts, psi, left, right, out, lefts, rights, own_row, prev_row, next_row, own_sum, sends, parts,
           load_sem, psi_sem, halo_send, halo_recv, part_send, part_recv):
    n, x = lax.axis_index("sec"), lax.axis_index("mpo")
    steps = len(TARGETS)
    targets = [entry(row, x) for row in TARGETS]
    sectors = [entry(row, x) for row in SECTORS]

    loads = []
    psi_load = pltpu.make_async_copy(psi.at[0], own_row, psi_sem)
    for k in range(steps):
        pair = (
            pltpu.make_async_copy(right.at[:, 0, targets[k]], rights.at[k], load_sem.at[0, k]),
            pltpu.make_async_copy(left.at[:, 0, targets[k]], lefts.at[k], load_sem.at[1, k]),
        )
        loads.append(pair)

    barrier = pltpu.get_barrier_semaphore()
    for distance in (1, 2, 3):
        pl.semaphore_signal(barrier, inc=1, device_id=(n, lax.rem(x + distance, 4)), device_id_type=MESH)

    @pl.when(n > 0)
    def _():
        pl.semaphore_signal(barrier, inc=1, device_id=(n - 1, x), device_id_type=MESH)

    @pl.when(n < rows - 1)
    def _():
        pl.semaphore_signal(barrier, inc=1, device_id=(n + 1, x), device_id_type=MESH)

    psi_load.start()
    for pair in loads:
        for load in pair:
            load.start()

    pl.semaphore_wait(barrier, 3 + (n + rows - 1) // rows + (2 * rows - 2 - n) // rows)

    def halo(k, side):
        return pltpu.make_async_remote_copy(
            src_ref=psi.at[0, sectors[k]],
            dst_ref=(prev_row, next_row)[side].at[sectors[k]],
            send_sem=halo_send.at[side, k],
            recv_sem=halo_recv.at[side, k],
            device_id=(n + 1 - 2 * side, x),
            device_id_type=MESH,
        )

    @pl.when(n < rows - 1)
    def _():
        for k in range(steps):
            halo(k, 0).start()

    @pl.when(n > 0)
    def _():
        for k in range(steps):
            halo(k, 1).start()

    def part(k):
        return pltpu.make_async_remote_copy(
            src_ref=sends.at[k],
            dst_ref=parts.at[lax.rem(targets[k] - x + 4, 4) - 1],
            send_sem=part_send.at[k],
            recv_sem=part_recv.at[lax.rem(targets[k] - x + 4, 4) - 1],
            device_id=(n, targets[k]),
            device_id_type=MESH,
        )

    psi_load.wait()
    for k in range(steps):
        t = targets[k]

        @pl.when(n > 0)
        def _():
            halo(k, 0).wait_recv()

        @pl.when(n < rows - 1)
        def _():
            halo(k, 1).wait_recv()

        for load in loads[k]:
            load.wait()
        first, last = (3 - t) // 3, t // 3
        low, high = t - 1 + 2 * first, t + 1 - 2 * last
        inner = []
        for w in range(4):
            row, col = shifts[w, 0], shifts[w, 1]
            outside = ((row > 0) & (n == 0)) | ((row < 0) & (n == rows - 1)) | ((col > 0) & (t == 0)) | ((col < 0) & (t == 3))
            below = jnp.where(col > 0, prev_row[low], prev_row[high])
            above = jnp.where(col > 0, next_row[low], next_row[high])
            source = jnp.where(row == 0, own_row[t], jnp.where(row > 0, below, above))
            source = jnp.where(outside, jnp.zeros_like(source), source)
            inner.append(dot(source, rights[k, w]).astype(bf16))
        total = sum(dot(lefts[k, w], inner[w]) for w in range(4))
        if k in (0, 3):
            own_sum[(targets[k] == x).astype(jnp.int32)] = total
        sends[k] = total.astype(bf16)

        @pl.when(t != x)
        def _():
            part(k).start()

    for slot in range(3):
        pltpu.make_async_remote_copy(
            src_ref=sends.at[0], dst_ref=parts.at[slot], send_sem=part_send.at[0], recv_sem=part_recv.at[slot],
            device_id=(n, lax.rem(x + 1, 4)), device_id_type=MESH,
        ).wait_recv()
    out[0, 0] = (own_sum[1] + parts[0].astype(f32) + parts[1].astype(f32) + parts[2].astype(f32)).astype(bf16)

    for k in range(steps):
        @pl.when(targets[k] != x)
        def _():
            part(k).wait_send()

        @pl.when(n < rows - 1)
        def _():
            halo(k, 0).wait_send()

        @pl.when(n > 0)
        def _():
            halo(k, 1).wait_send()


def per_device(rows, psi, left_env, right_env, shifts):
    terms, _, sectors, width, _ = left_env.shape
    block = (width, width)
    return pl.pallas_call(
        functools.partial(kernel, rows),
        out_shape=jax.ShapeDtypeStruct((1, 1) + block, bf16),
        in_specs=[pl.BlockSpec(memory_space=pltpu.SMEM)] + [pl.BlockSpec(memory_space=pl.ANY)] * 3,
        out_specs=pl.BlockSpec(memory_space=pltpu.VMEM),
        scratch_shapes=[
            pltpu.VMEM((sectors, terms) + block, bf16),
            pltpu.VMEM((sectors, terms) + block, bf16),
            pltpu.VMEM((sectors,) + block, bf16),
            pltpu.VMEM((sectors,) + block, bf16),
            pltpu.VMEM((sectors,) + block, bf16),
            pltpu.VMEM((2,) + block, f32),
            pltpu.VMEM((sectors,) + block, bf16),
            pltpu.VMEM((3,) + block, bf16),
            pltpu.SemaphoreType.DMA((2, sectors)),
            pltpu.SemaphoreType.DMA,
            pltpu.SemaphoreType.DMA((2, sectors)),
            pltpu.SemaphoreType.DMA((2, sectors)),
            pltpu.SemaphoreType.DMA((sectors,)),
            pltpu.SemaphoreType.DMA((3,)),
        ],
        compiler_params=pltpu.CompilerParams(collective_id=0, has_side_effects=True, vmem_limit_bytes=56 << 20),
        cost_estimate=pl.CostEstimate(flops=4 * terms * sectors * width**3, bytes_accessed=36 << 20, transcendentals=0),
    )(shifts, psi, left_env, right_env)


def solution(mesh):
    return jax.shard_map(
        functools.partial(per_device, mesh.shape["sec"]),
        mesh=mesh,
        in_specs=(
            P("sec", None, None, None),
            P("mpo", "sec", None, None, None),
            P("mpo", "sec", None, None, None),
            P("mpo", None),
        ),
        out_specs=P("sec", "mpo", None, None),
        check_vma=False,
    )
```

```python
import functools

import jax
import jax.numpy as jnp
from jax import lax
from jax.experimental import pallas as pl
from jax.experimental.pallas import tpu as pltpu
from jax.sharding import PartitionSpec as P

MESH = pl.DeviceIdType.MESH
f32, bf16 = jnp.float32, jnp.bfloat16
dot = functools.partial(jnp.dot, preferred_element_type=f32)

SECTORS = ((1, 1, 2, 2), (3, 2, 1, 0), (2, 3, 0, 1), (0, 0, 3, 3))
TARGETS = ((2, 3, 0, 1), (0, 0, 3, 3), (3, 2, 1, 0), (1, 1, 2, 2))
STEPS, TERMS, HALF, QUARTER = 4, 4, 256, 128


def entry(row, x):
    code = sum(value * 4**i for i, value in enumerate(row))
    power = (1 + 3 * lax.rem(x, 2)) * (1 + 15 * (x // 2))
    return lax.rem(code // power, 4)


def rows_at(start, size):
    return pl.ds(pl.multiple_of(start, size), size)


def kernel(rows, shifts, psi, left, right, out, lefts, rights, own_row, far_row, near_row, acc, own_sum, sends, parts,
           left_sem, right_sem, psi_sem, far_send, far_recv, near_send, near_recv, swap_send, swap_recv, part_send, part_recv):
    n, x = lax.axis_index("sec"), lax.axis_index("mpo")
    core, mine = lax.rem(n, 2), lax.rem(x, 2)
    near, far, pair = n + 1 - 2 * core, n - 1 + 2 * core, x + 1 - 2 * mine
    inside = (far >= 0) & (far < rows)
    sectors = [entry(row, x) for row in SECTORS]
    targets = [entry(row, x) for row in TARGETS]
    halves = (mine, 1 - mine)

    psi_load = pltpu.make_async_copy(psi.at[0], own_row, psi_sem)
    right_load = [pltpu.make_async_copy(right.at[:, 0, targets[k]], rights.at[k], right_sem.at[k]) for k in range(STEPS)]
    left_load = [
        [pltpu.make_async_copy(left.at[:, 0, targets[k], :, rows_at(halves[i] * HALF, HALF)], lefts.at[k, i], left_sem.at[k, i]) for i in range(2)]
        for k in range(STEPS)
    ]

    def remote(src, dst, send, recv, device):
        return pltpu.make_async_remote_copy(src_ref=src, dst_ref=dst, send_sem=send, recv_sem=recv, device_id=device, device_id_type=MESH)

    def far_copy(k, i):
        span = rows_at(mine * HALF + i * QUARTER, QUARTER) if k == 0 else rows_at(halves[i] * HALF, HALF)
        return remote(psi.at[0, sectors[k], span], far_row.at[sectors[k], span], far_send.at[k, i], far_recv.at[k, i], (far, x))

    def near_copy(k):
        return remote(psi.at[0, sectors[k]], near_row.at[sectors[k]], near_send.at[k], near_recv.at[k], (near, x))

    def swap_copy(half, i):
        span = rows_at(half * HALF + i * QUARTER, QUARTER)
        there = far_row.at[sectors[0], span]
        return remote(there, there, swap_send.at[i], swap_recv.at[i], (n, pair))

    def part_copy(k, r):
        slot = lax.rem(targets[k] - x + 4, 4) - 1
        span = pl.ds(r * HALF, HALF)
        return remote(sends.at[k, span], parts.at[slot, span], part_send.at[k, r], part_recv.at[slot, r], (n, targets[k]))

    barrier = pltpu.get_barrier_semaphore()
    for device in ((near, x), (n, lax.rem(x + 1, 4)), (n, lax.rem(x + 2, 4)), (n, lax.rem(x + 3, 4))):
        pl.semaphore_signal(barrier, inc=1, device_id=device, device_id_type=MESH)

    @pl.when(inside)
    def _():
        pl.semaphore_signal(barrier, inc=1, device_id=(far, x), device_id_type=MESH)

    psi_load.start()
    for k in range(STEPS):
        right_load[k].start()
        left_load[k][0].start()
        left_load[k][1].start()

    pl.semaphore_wait(barrier, 4 + ((n + rows - 1) // rows) * ((2 * rows - 2 - n) // rows))

    @pl.when(inside)
    def _():
        for k in range(STEPS):
            for i in range(2):
                far_copy(k, i).start()

    for k in range(STEPS):
        near_copy(k).start()

    @pl.when(inside)
    def _():
        for i in range(2):
            far_copy(0, i).wait_recv()
            swap_copy(mine, i).start()

    def source(w, t, half):
        first, last = (3 - t) // 3, t // 3
        low, high = t - 1 + 2 * first, t + 1 - 2 * last
        span = rows_at(half * HALF, HALF)
        row, col = shifts[0, w], shifts[1, w]
        outside = ((row > 0) & (n == 0)) | ((row < 0) & (n == rows - 1)) | ((col > 0) & (t == 0)) | ((col < 0) & (t == 3))
        from_far = (row > 0) == (core == 0)
        away = jnp.where(from_far, jnp.where(col > 0, far_row[low, span], far_row[high, span]),
                         jnp.where(col > 0, near_row[low, span], near_row[high, span]))
        block = jnp.where(row == 0, own_row[t, span], away)
        return jnp.where(outside, jnp.zeros_like(block), block)

    def products(k, i):
        return [dot(source(w, targets[k], halves[i]), rights[k, w]).astype(bf16) for w in range(TERMS)]

    def first_half(k):
        right_load[k].wait()
        left_load[k][0].wait()
        inner = products(k, 0)
        acc[...] = sum(dot(lefts[k, 0, w], inner[w]) for w in range(TERMS))

    def second_half(k, ready):
        left_load[k][1].wait()
        inner = products(k, 1)
        for r in range(2):
            span = pl.ds(r * HALF, HALF)
            total = acc[span] + sum(dot(lefts[k, 1, w, span], inner[w]) for w in range(TERMS))
            if k in (1, 3):
                own_sum[(targets[k] == x).astype(jnp.int32), span] = total
            sends[k, span] = total.astype(bf16)
            ready(r)

    def send(k, r):
        if k in (1, 3):
            pl.when(targets[k] != x)(part_copy(k, r).start)
        else:
            part_copy(k, r).start()

    def arrived(k, i):
        pl.when(inside)(far_copy(k, i).wait_recv)

    psi_load.wait()
    near_copy(0).wait_recv()
    near_copy(1).wait_recv()
    arrived(1, 0)
    first_half(0)
    arrived(1, 1)

    @pl.when(inside)
    def _():
        for i in range(2):
            swap_copy(1 - mine, i).wait_recv()

    second_half(0, lambda r: send(0, r))

    first_half(1)
    second_half(1, lambda r: None)

    near_copy(2).wait_recv()
    arrived(2, 0)
    first_half(2)
    arrived(2, 1)
    second_half(2, lambda r: None)

    near_copy(3).wait_recv()
    arrived(3, 0)
    first_half(3)
    for r in range(2):
        send(1, r)
        send(2, r)
    arrived(3, 1)
    second_half(3, lambda r: send(3, r))

    for r in range(2):
        span = pl.ds(r * HALF, HALF)
        for slot in (1, 0, 2):
            remote(sends.at[0, span], parts.at[slot, span], part_send.at[0, r], part_recv.at[slot, r], (n, pair)).wait_recv()
        out[0, 0, span] = (own_sum[1, span] + parts[0, span].astype(f32) + parts[1, span].astype(f32) + parts[2, span].astype(f32)).astype(bf16)

    for k in range(STEPS):
        near_copy(k).wait_send()
        for i in range(2):
            pl.when(inside)(far_copy(k, i).wait_send)
            if k in (1, 3):
                pl.when(targets[k] != x)(part_copy(k, i).wait_send)
            else:
                part_copy(k, i).wait_send()
    for i in range(2):
        pl.when(inside)(swap_copy(mine, i).wait_send)


def per_device(rows, psi, left_env, right_env, shifts):
    terms, _, sectors, width, _ = left_env.shape
    block = (width, width)
    pairs = pltpu.SemaphoreType.DMA((STEPS, 2))
    singles = pltpu.SemaphoreType.DMA((STEPS,))
    return pl.pallas_call(
        functools.partial(kernel, rows),
        out_shape=pltpu.VMEM((1, 1) + block, bf16),
        in_specs=[pl.BlockSpec(memory_space=pltpu.SMEM)] + [pl.BlockSpec(memory_space=pl.ANY)] * 3,
        out_specs=pl.BlockSpec(memory_space=pltpu.VMEM),
        scratch_shapes=[
            pltpu.VMEM((STEPS, 2, terms, width, HALF), bf16),
            pltpu.VMEM((STEPS, terms) + block, bf16),
            pltpu.VMEM((sectors,) + block, bf16),
            pltpu.VMEM((sectors,) + block, bf16),
            pltpu.VMEM((sectors,) + block, bf16),
            pltpu.VMEM(block, f32),
            pltpu.VMEM((2,) + block, f32),
            pltpu.VMEM((STEPS,) + block, bf16),
            pltpu.VMEM((3,) + block, bf16),
            pairs,
            singles,
            pltpu.SemaphoreType.DMA,
            pairs,
            pairs,
            singles,
            singles,
            pltpu.SemaphoreType.DMA((2,)),
            pltpu.SemaphoreType.DMA((2,)),
            pairs,
            pltpu.SemaphoreType.DMA((3, 2)),
        ],
        compiler_params=pltpu.CompilerParams(collective_id=0, has_side_effects=True, vmem_limit_bytes=56 << 20),
        cost_estimate=pl.CostEstimate(flops=4 * terms * sectors * width**3, bytes_accessed=36 << 20, transcendentals=0),
    )(shifts.T, psi, left_env, right_env)


def solution(mesh):
    return jax.shard_map(
        functools.partial(per_device, mesh.shape["sec"]),
        mesh=mesh,
        in_specs=(
            P("sec", None, None, None),
            P("mpo", "sec", None, None, None),
            P("mpo", "sec", None, None, None),
            P("mpo", None),
        ),
        out_specs=P("sec", "mpo", None, None),
        check_vma=False,
    )
```

```python
import functools

import jax
import jax.numpy as jnp
from jax import lax
from jax.experimental import pallas as pl
from jax.experimental.pallas import tpu as pltpu
from jax.sharding import PartitionSpec as P

MESH = pl.DeviceIdType.MESH
f32, bf16 = jnp.float32, jnp.bfloat16
dot = functools.partial(jnp.dot, preferred_element_type=f32)

SECTORS = (2, 1, 0, 3)
TARGETS = ((3, 3, 3, 3), (1, 1, 1, 1), (2, 2, 0, 2), (0, 0, 2, 0))
STEP_OWN, STEP_UP, STEP_DOWN = (3, 1, 3, 0), (1, 2, 0, 3), (0, 3, 1, 2)
STEPS, TERMS, HALF, QUARTER, EIGHTH = 4, 4, 256, 128, 64


def entry(row, x):
    code = sum(value * 4**i for i, value in enumerate(row))
    power = (1 + 3 * lax.rem(x, 2)) * (1 + 15 * (x // 2))
    return lax.rem(code // power, 4)


def rows_at(start, size):
    return pl.ds(pl.multiple_of(start, size), size)


def kernel(rows, shifts, psi, left, right, out, lefts, rights, own_row, far_row, near_row, sums, sends, middle, parts,
           left_sem, right_sem, psi_sem, far_send, far_recv, near_send, near_recv, hop1_send, hop1_recv, hop2_send, hop2_recv,
           mid_send, mid_recv, whole_send, whole_recv, added_send, added_recv):
    n, x = lax.axis_index("sec"), lax.axis_index("mpo")
    core = lax.rem(n, 2)
    near, far = n + 1 - 2 * core, n - 1 + 2 * core
    beside = (lax.rem(x + 1, 4), lax.rem(x + 3, 4))
    inside = (far >= 0) & (far < rows)
    targets = [row[0] if len(set(row)) == 1 else entry(row, x) for row in TARGETS]
    steps, own = (entry(STEP_UP, x), entry(STEP_DOWN, x)), entry(STEP_OWN, x)

    psi_load = pltpu.make_async_copy(psi.at[0], own_row, psi_sem)
    right_load = [pltpu.make_async_copy(right.at[:, 0, targets[k]], rights.at[k], right_sem.at[k]) for k in range(STEPS)]
    left_load = [
        [pltpu.make_async_copy(left.at[:, 0, targets[k], :, pl.ds(i * HALF, HALF)], lefts.at[k, i], left_sem.at[k, i]) for i in range(2)]
        for k in range(STEPS)
    ]

    def remote(src, dst, send, recv, device):
        return pltpu.make_async_remote_copy(src_ref=src, dst_ref=dst, send_sem=send, recv_sem=recv, device_id=device, device_id_type=MESH)

    def far_copy(k, i):
        span = rows_at(x * QUARTER + i * EIGHTH, EIGHTH) if k < 2 else pl.ds(i * HALF, HALF)
        return remote(psi.at[0, SECTORS[k], span], far_row.at[SECTORS[k], span], far_send.at[k, i], far_recv.at[k, i], (far, x))

    def near_copy(k):
        return remote(psi.at[0, SECTORS[k]], near_row.at[SECTORS[k]], near_send.at[k], near_recv.at[k], (near, x))

    def hop1(k, side, piece, owner):
        there = far_row.at[SECTORS[k], rows_at(owner * QUARTER + (piece ^ side) * EIGHTH, EIGHTH)]
        return remote(there, there, hop1_send.at[k, side, piece], hop1_recv.at[k, side, piece], (n, beside[side]))

    def hop2(k, side, owner):
        there = far_row.at[SECTORS[k], rows_at(owner * QUARTER + side * EIGHTH, EIGHTH)]
        return remote(there, there, hop2_send.at[k, side], hop2_recv.at[k, side], (n, beside[side]))

    def mid_copy(k, side, c):
        there = sends.at[k, pl.ds(side * HALF + c * QUARTER, QUARTER)]
        return remote(there, middle.at[side, pl.ds(c * QUARTER, QUARTER)], mid_send.at[side, c], mid_recv.at[side, c], (n, beside[side]))

    def whole_copy(k, side):
        span = pl.ds((1 - side) * HALF, HALF)
        return remote(sends.at[k, span], parts.at[side, span], whole_send.at[side], whole_recv.at[side], (n, beside[side]))

    def added_copy(side, c):
        span = pl.ds(side * HALF + c * QUARTER, QUARTER)
        return remote(sends.at[steps[side], span], parts.at[side, span], added_send.at[side, c], added_recv.at[side, c], (n, beside[side]))

    barrier = pltpu.get_barrier_semaphore()
    for device in ((near, x), (n, beside[0]), (n, beside[1])):
        pl.semaphore_signal(barrier, inc=1, device_id=device, device_id_type=MESH)

    @pl.when(inside)
    def _():
        pl.semaphore_signal(barrier, inc=1, device_id=(far, x), device_id_type=MESH)

    psi_load.start()
    for k in range(STEPS):
        right_load[k].start()
        left_load[k][0].start()
        left_load[k][1].start()

    pl.semaphore_wait(barrier, 3 + ((n + rows - 1) // rows) * ((2 * rows - 2 - n) // rows))

    @pl.when(inside)
    def _():
        for k in range(STEPS):
            for i in range(2):
                far_copy(k, i).start()

    for k in (0, 2, 1, 3):
        near_copy(k).start()

    def spread(k):
        for side in range(2):
            far_copy(k, side).wait_recv()
            hop1(k, side, 0, x).start()
        for side in range(2):
            hop1(k, side, 1, x).start()

    def pass_on(k):
        for side in range(2):
            hop1(k, side, 0, beside[1 - side]).wait_recv()
            hop2(k, side, beside[1 - side]).start()

    @pl.when(inside)
    def _():
        spread(0)
        pass_on(0)
        spread(1)

    def source(w, t, half):
        first, last = (3 - t) // 3, t // 3
        low, high = t - 1 + 2 * first, t + 1 - 2 * last
        span = pl.ds(half * HALF, HALF)
        row, col = shifts[0, w], shifts[1, w]
        outside = ((row > 0) & (n == 0)) | ((row < 0) & (n == rows - 1)) | ((col > 0) & (t == 0)) | ((col < 0) & (t == 3))
        from_far = (row > 0) == (core == 0)
        away = jnp.where(from_far, jnp.where(col > 0, far_row[low, span], far_row[high, span]),
                         jnp.where(col > 0, near_row[low, span], near_row[high, span]))
        block = jnp.where(row == 0, own_row[t, span], away)
        return jnp.where(outside, jnp.zeros_like(block), block)

    def products(k, i):
        return [dot(source(w, targets[k], i), rights[k, w]).astype(bf16) for w in range(TERMS)]

    def first_half(k):
        right_load[k].wait()
        left_load[k][0].wait()
        inner = products(k, 0)
        sums[k] = sum(dot(lefts[k, 0, w], inner[w]) for w in range(TERMS))

    def second_half(k):
        left_load[k][1].wait()
        inner = products(k, 1)
        for r in range(2):
            span = pl.ds(r * HALF, HALF)
            total = sums[k, span] + sum(dot(lefts[k, 1, w, span], inner[w]) for w in range(TERMS))
            sums[k, span] = total
            sends[k, span] = total.astype(bf16)

            @pl.when(targets[k] == lax.rem(x + 2, 4))
            def _():
                for c in range(2):
                    mid_copy(k, r, c).start()

            pl.when(targets[k] == beside[1 - r])(whole_copy(k, 1 - r).start)

    def arrived(k, i, where):
        pl.when(where)(far_copy(k, i).wait_recv)

    def gathered(k):
        @pl.when(inside)
        def _():
            for side in range(2):
                hop1(k, side, 1, beside[1 - side]).wait_recv()
                hop2(k, side, lax.rem(x + 2, 4)).wait_recv()

    psi_load.wait()
    near_copy(0).wait_recv()
    gathered(0)
    first_half(0)
    pl.when(inside)(functools.partial(pass_on, 1))
    second_half(0)

    near_copy(2).wait_recv()
    for i in range(2):
        arrived(2, i, inside)
    first_half(1)
    second_half(1)

    for k in (1, 3):
        near_copy(k).wait_recv()
    gathered(1)
    early = inside & (x != 2)
    arrived(3, 0, early)
    first_half(2)
    arrived(3, 1, early)
    second_half(2)

    for i in range(2):
        arrived(3, i, inside & (x == 2))
    first_half(3)
    second_half(3)

    for c in range(2):
        for side in range(2):
            if c == 0:
                for i in range(2):
                    mid_copy(0, side, i).wait_send()
            mid_copy(0, side, c).wait_recv()
            span = pl.ds(side * HALF + c * QUARTER, QUARTER)
            sends[steps[side], span] = (sums[steps[side], span] + middle[side, pl.ds(c * QUARTER, QUARTER)].astype(f32)).astype(bf16)
            added_copy(side, c).start()

    for side in range(2):
        whole_copy(0, side).wait_recv()
    for c in range(2):
        for side in range(2):
            added_copy(side, c).wait_recv()
            span = pl.ds(side * HALF + c * QUARTER, QUARTER)
            out[0, 0, span] = (sums[own, span] + parts[0, span].astype(f32) + parts[1, span].astype(f32)).astype(bf16)

    for k in range(STEPS):
        near_copy(k).wait_send()
    for side in range(2):
        whole_copy(0, side).wait_send()
        for c in range(2):
            added_copy(side, c).wait_send()

    @pl.when(inside)
    def _():
        for k in range(STEPS):
            for i in range(2):
                far_copy(k, i).wait_send()
        for k in range(2):
            for side in range(2):
                hop2(k, side, x).wait_send()
                for piece in range(2):
                    hop1(k, side, piece, x).wait_send()


def per_device(rows, psi, left_env, right_env, shifts):
    terms, _, sectors, width, _ = left_env.shape
    block = (width, width)
    pairs = pltpu.SemaphoreType.DMA((STEPS, 2))
    singles = pltpu.SemaphoreType.DMA((STEPS,))
    return pl.pallas_call(
        functools.partial(kernel, rows),
        out_shape=pltpu.VMEM((1, 1) + block, bf16),
        in_specs=[pl.BlockSpec(memory_space=pltpu.SMEM)] + [pl.BlockSpec(memory_space=pl.ANY)] * 3,
        out_specs=pl.BlockSpec(memory_space=pltpu.VMEM),
        scratch_shapes=[
            pltpu.VMEM((STEPS, 2, terms, width, HALF), bf16),
            pltpu.VMEM((STEPS, terms) + block, bf16),
            pltpu.VMEM((sectors,) + block, bf16),
            pltpu.VMEM((sectors,) + block, bf16),
            pltpu.VMEM((sectors,) + block, bf16),
            pltpu.VMEM((STEPS,) + block, f32),
            pltpu.VMEM((STEPS,) + block, bf16),
            pltpu.VMEM((2, HALF, width), bf16),
            pltpu.VMEM((2,) + block, bf16),
            pairs,
            singles,
            pltpu.SemaphoreType.DMA,
            pairs,
            pairs,
            singles,
            singles,
        ] + [pltpu.SemaphoreType.DMA((2, 2, 2))] * 2 + [pltpu.SemaphoreType.DMA((2, 2))] * 4 + [pltpu.SemaphoreType.DMA((2,))] * 2 + [pltpu.SemaphoreType.DMA((2, 2))] * 2,
        compiler_params=pltpu.CompilerParams(collective_id=0, has_side_effects=True, vmem_limit_bytes=56 << 20),
        cost_estimate=pl.CostEstimate(flops=4 * terms * sectors * width**3, bytes_accessed=36 << 20, transcendentals=0),
    )(shifts.T, psi, left_env, right_env)


def solution(mesh):
    return jax.shard_map(
        functools.partial(per_device, mesh.shape["sec"]),
        mesh=mesh,
        in_specs=(
            P("sec", None, None, None),
            P("mpo", "sec", None, None, None),
            P("mpo", "sec", None, None, None),
            P("mpo", None),
        ),
        out_specs=P("sec", "mpo", None, None),
        check_vma=False,
    )
```

```python
import functools

import jax
import jax.numpy as jnp
from jax import lax
from jax.experimental import pallas as pl
from jax.experimental.pallas import tpu as pltpu
from jax.sharding import PartitionSpec as P

MESH = pl.DeviceIdType.MESH
f32, bf16 = jnp.float32, jnp.bfloat16
dot = functools.partial(jnp.dot, preferred_element_type=f32)

SECTORS = (2, 1, 0, 3)
TARGETS = ((3, 3, 3, 1), (1, 0, 1, 0), (2, 2, 0, 2), (0, 1, 2, 3))
STEP_UP, STEP_DOWN = (1, 2, 0, 1), (0, 1, 1, 2)
STEPS, TERMS, HALF, QUARTER, EIGHTH = 4, 4, 256, 128, 64


def entry(row, x):
    code = sum(value * 4**i for i, value in enumerate(row))
    power = (1 + 3 * lax.rem(x, 2)) * (1 + 15 * (x // 2))
    return lax.rem(code // power, 4)


def rows_at(start, size):
    return pl.ds(pl.multiple_of(start, size), size)


def kernel(rows, shifts, psi, left, right, out, lefts, rights, own_row, far_row, near_row, sums, sends, middle, parts,
           left_sem, right_sem, psi_sem, far_send, far_recv, near_send, near_recv, hop1_send, hop1_recv, hop2_send, hop2_recv, share_send, share_recv,
           mid_send, mid_recv, whole_send, whole_recv, added_send, added_recv):
    n, x = lax.axis_index("sec"), lax.axis_index("mpo")
    core = lax.rem(n, 2)
    near, far = n + 1 - 2 * core, n - 1 + 2 * core
    beside = (lax.rem(x + 1, 4), lax.rem(x + 3, 4))
    inside = (far >= 0) & (far < rows)
    targets, steps = [entry(row, x) for row in TARGETS], (entry(STEP_UP, x), entry(STEP_DOWN, x))

    psi_load = pltpu.make_async_copy(psi.at[0], own_row, psi_sem)
    right_load = [pltpu.make_async_copy(right.at[:, 0, targets[k]], rights.at[k], right_sem.at[k]) for k in range(STEPS)]
    left_load = [
        [pltpu.make_async_copy(left.at[:, 0, targets[k], :, pl.ds(i * HALF, HALF)], lefts.at[k, i], left_sem.at[k, i]) for i in range(2)]
        for k in range(STEPS)
    ]

    def remote(src, dst, send, recv, device):
        return pltpu.make_async_remote_copy(src_ref=src, dst_ref=dst, send_sem=send, recv_sem=recv, device_id=device, device_id_type=MESH)

    def far_copy(k, i):
        if k == 0:
            span = rows_at(x * QUARTER + i * EIGHTH, EIGHTH)
        elif k == 1:
            span = rows_at(lax.rem(x + 2 * i, 4) * QUARTER, QUARTER)
        else:
            span = pl.ds(i * HALF, HALF)
        return remote(psi.at[0, SECTORS[k], span], far_row.at[SECTORS[k], span], far_send.at[k, i], far_recv.at[k, i], (far, x))

    def near_copy(k):
        return remote(psi.at[0, SECTORS[k]], near_row.at[SECTORS[k]], near_send.at[k], near_recv.at[k], (near, x))

    def hop1(side, piece, owner):
        there = far_row.at[SECTORS[0], rows_at(owner * QUARTER + (piece ^ side) * EIGHTH, EIGHTH)]
        return remote(there, there, hop1_send.at[side, piece], hop1_recv.at[side, piece], (n, beside[side]))

    def hop2(side, owner):
        there = far_row.at[SECTORS[0], rows_at(owner * QUARTER + side * EIGHTH, EIGHTH)]
        return remote(there, there, hop2_send.at[side], hop2_recv.at[side], (n, beside[side]))

    def share(side, owner):
        there = far_row.at[SECTORS[1], rows_at(owner * QUARTER, QUARTER)]
        return remote(there, there, share_send.at[side], share_recv.at[side], (n, beside[side]))

    def mid_copy(k, side, c):
        there = sends.at[k, pl.ds(side * HALF + c * QUARTER, QUARTER)]
        return remote(there, middle.at[side, pl.ds(c * QUARTER, QUARTER)], mid_send.at[side, c], mid_recv.at[side, c], (n, beside[side]))

    def whole_copy(k, side):
        span = pl.ds((1 - side) * HALF, HALF)
        return remote(sends.at[k, span], parts.at[side, span], whole_send.at[side], whole_recv.at[side], (n, beside[side]))

    def added_copy(side, c):
        span = pl.ds(side * HALF + c * QUARTER, QUARTER)
        return remote(sends.at[steps[side], span], parts.at[side, span], added_send.at[side, c], added_recv.at[side, c], (n, beside[side]))

    barrier = pltpu.get_barrier_semaphore()
    for device in ((near, x), (n, beside[0]), (n, beside[1])):
        pl.semaphore_signal(barrier, inc=1, device_id=device, device_id_type=MESH)

    @pl.when(inside)
    def _():
        pl.semaphore_signal(barrier, inc=1, device_id=(far, x), device_id_type=MESH)

    psi_load.start()
    for k in range(STEPS):
        right_load[k].start()
        left_load[k][0].start()
        left_load[k][1].start()

    pl.semaphore_wait(barrier, 3 + ((n + rows - 1) // rows) * ((2 * rows - 2 - n) // rows))

    @pl.when(inside)
    def _():
        for k, i in ((0, 0), (0, 1), (1, 0), (2, 0), (2, 1), (1, 1), (3, 0), (3, 1)):
            far_copy(k, i).start()

    for k in (0, 2, 1, 3):
        near_copy(k).start()

    @pl.when(inside)
    def _():
        for side in range(2):
            far_copy(0, side).wait_recv()
            hop1(side, 0, x).start()
        for side in range(2):
            hop1(side, 1, x).start()
        for side in range(2):
            hop1(side, 0, beside[1 - side]).wait_recv()
            hop2(side, beside[1 - side]).start()
        far_copy(1, 0).wait_recv()
        for side in range(2):
            share(side, x).start()

    def source(w, t, span):
        first, last = (3 - t) // 3, t // 3
        low, high = t - 1 + 2 * first, t + 1 - 2 * last
        row, col = shifts[0, w], shifts[1, w]
        outside = ((row > 0) & (n == 0)) | ((row < 0) & (n == rows - 1)) | ((col > 0) & (t == 0)) | ((col < 0) & (t == 3))
        from_far = (row > 0) == (core == 0)
        away = jnp.where(from_far, jnp.where(col > 0, far_row[low, span], far_row[high, span]),
                         jnp.where(col > 0, near_row[low, span], near_row[high, span]))
        block = jnp.where(row == 0, own_row[t, span], away)
        return jnp.where(outside, jnp.zeros_like(block), block)

    def products(k, span):
        return [dot(source(w, targets[k], span), rights[k, w]).astype(bf16) for w in range(TERMS)]

    def order(k):
        up = (targets[k] == beside[0]).astype(jnp.int32) if k < 3 else 0
        return (up, 1 - up)

    def keep(k, span, total):
        sums[k, span] = total
        if k < 3:
            sends[k, span] = total.astype(bf16)

    def send(k, r):
        @pl.when(targets[k] == lax.rem(x + 2, 4))
        def _():
            for c in range(2):
                mid_copy(k, r, c).start()

        if r == 0:
            for side in range(2):
                pl.when(targets[k] == beside[side])(whole_copy(k, side).start)

    def first_half(k):
        right_load[k].wait()
        left_load[k][0].wait()
        inner = products(k, pl.ds(0, HALF))
        sums[k] = sum(dot(lefts[k, 0, w], inner[w]) for w in range(TERMS))

    def second_half(k):
        left_load[k][1].wait()
        inner = products(k, pl.ds(HALF, HALF))
        for r, half in enumerate(order(k)):
            span = rows_at(half * HALF, HALF)
            keep(k, span, sums[k, span] + sum(dot(lefts[k, 1, w, span], inner[w]) for w in range(TERMS)))
            if k < 3:
                send(k, r)

    def at_once(k):
        right_load[k].wait()
        left_load[k][0].wait()
        left_load[k][1].wait()
        inner = products(k, pl.ds(0, 2 * HALF))
        for r, half in enumerate(order(k)):
            span = rows_at(half * HALF, HALF)
            keep(k, span, sum(dot(lefts[k, i, w, span], inner[w][i * HALF:(i + 1) * HALF]) for w in range(TERMS) for i in range(2)))
            if k < 3:
                send(k, r)

    def arrived(k, i, where):
        pl.when(inside & where)(far_copy(k, i).wait_recv)

    psi_load.wait()
    for k in range(STEPS):
        near_copy(k).wait_recv()

    @pl.when(inside)
    def _():
        for side in range(2):
            hop1(side, 1, beside[1 - side]).wait_recv()
            hop2(side, lax.rem(x + 2, 4)).wait_recv()

    arrived(2, 0, x == 3)
    arrived(2, 1, x == 3)
    at_once(0)

    arrived(1, 1, x >= 0)
    arrived(2, 0, x != 3)
    arrived(2, 1, x != 3)

    @pl.when(inside)
    def _():
        for side in range(2):
            share(side, beside[1 - side]).wait_recv()

    at_once(1)

    arrived(3, 0, x != 2)
    first_half(2)
    arrived(3, 1, x != 2)
    second_half(2)

    arrived(3, 0, x == 2)
    arrived(3, 1, x == 2)
    at_once(3)

    for c in range(2):
        for side in range(2):
            if c == 0:
                for i in range(2):
                    mid_copy(0, side, i).wait_send()
            mid_copy(0, side, c).wait_recv()
            span = pl.ds(side * HALF + c * QUARTER, QUARTER)
            sends[steps[side], span] = (sums[steps[side], span] + middle[side, pl.ds(c * QUARTER, QUARTER)].astype(f32)).astype(bf16)
            added_copy(side, c).start()

    for side in range(2):
        whole_copy(0, side).wait_recv()
    for c in range(2):
        for side in range(2):
            added_copy(side, c).wait_recv()
            span = pl.ds(side * HALF + c * QUARTER, QUARTER)
            out[0, 0, span] = (sums[3, span] + parts[0, span].astype(f32) + parts[1, span].astype(f32)).astype(bf16)

    for k in range(STEPS):
        near_copy(k).wait_send()
    for side in range(2):
        whole_copy(0, side).wait_send()
        for c in range(2):
            added_copy(side, c).wait_send()

    @pl.when(inside)
    def _():
        for k in range(STEPS):
            for i in range(2):
                far_copy(k, i).wait_send()
        for side in range(2):
            share(side, x).wait_send()
            hop2(side, x).wait_send()
            for piece in range(2):
                hop1(side, piece, x).wait_send()


def per_device(rows, psi, left_env, right_env, shifts):
    terms, _, sectors, width, _ = left_env.shape
    block = (width, width)
    pairs = pltpu.SemaphoreType.DMA((STEPS, 2))
    singles = pltpu.SemaphoreType.DMA((STEPS,))
    return pl.pallas_call(
        functools.partial(kernel, rows),
        out_shape=pltpu.VMEM((1, 1) + block, bf16),
        in_specs=[pl.BlockSpec(memory_space=pltpu.SMEM)] + [pl.BlockSpec(memory_space=pl.ANY)] * 3,
        out_specs=pl.BlockSpec(memory_space=pltpu.VMEM),
        scratch_shapes=[
            pltpu.VMEM((STEPS, 2, terms, width, HALF), bf16),
            pltpu.VMEM((STEPS, terms) + block, bf16),
            pltpu.VMEM((sectors,) + block, bf16),
            pltpu.VMEM((sectors,) + block, bf16),
            pltpu.VMEM((sectors,) + block, bf16),
            pltpu.VMEM((STEPS,) + block, f32),
            pltpu.VMEM((STEPS,) + block, bf16),
            pltpu.VMEM((2, HALF, width), bf16),
            pltpu.VMEM((2,) + block, bf16),
            pairs,
            singles,
            pltpu.SemaphoreType.DMA,
            pairs,
            pairs,
            singles,
            singles,
        ] + [pltpu.SemaphoreType.DMA((2, 2))] * 2 + [pltpu.SemaphoreType.DMA((2,))] * 4 + [pltpu.SemaphoreType.DMA((2, 2))] * 2 + [pltpu.SemaphoreType.DMA((2,))] * 2 + [pltpu.SemaphoreType.DMA((2, 2))] * 2,
        compiler_params=pltpu.CompilerParams(collective_id=0, has_side_effects=True, vmem_limit_bytes=56 << 20),
        cost_estimate=pl.CostEstimate(flops=4 * terms * sectors * width**3, bytes_accessed=36 << 20, transcendentals=0),
    )(shifts.T, psi, left_env, right_env)


def solution(mesh):
    return jax.shard_map(
        functools.partial(per_device, mesh.shape["sec"]),
        mesh=mesh,
        in_specs=(
            P("sec", None, None, None),
            P("mpo", "sec", None, None, None),
            P("mpo", "sec", None, None, None),
            P("mpo", None),
        ),
        out_specs=P("sec", "mpo", None, None),
        check_vma=False,
    )
```

```python
import functools

import jax
import jax.numpy as jnp
from jax import lax
from jax.experimental import pallas as pl
from jax.experimental.pallas import tpu as pltpu
from jax.sharding import PartitionSpec as P

MESH = pl.DeviceIdType.MESH
f32, bf16 = jnp.float32, jnp.bfloat16
dot = functools.partial(jnp.dot, preferred_element_type=f32)

SECTORS = (2, 1, 0, 3)
TARGETS = ((3, 3, 3, 1), (1, 0, 1, 0), (2, 2, 0, 2), (0, 1, 2, 3))
STEP_UP, STEP_DOWN = (1, 2, 0, 1), (0, 1, 1, 2)
STEPS, TERMS, HALF, QUARTER, EIGHTH = 4, 4, 256, 128, 64


def entry(row, x):
    code = sum(value * 4**i for i, value in enumerate(row))
    power = (1 + 3 * lax.rem(x, 2)) * (1 + 15 * (x // 2))
    return lax.rem(code // power, 4)


def rows_at(start, size):
    return pl.ds(pl.multiple_of(start, size), size)


def kernel(rows, shifts, psi, left, right, out, lefts, rights, own_row, far_row, near_row, sums, sends, middle, parts,
           left_sem, right_sem, psi_sem, far_send, far_recv, near_send, near_recv, hop1_send, hop1_recv, hop2_send, hop2_recv, share_send, share_recv,
           mid_send, mid_recv, whole_send, whole_recv, added_send, added_recv):
    n, x = lax.axis_index("sec"), lax.axis_index("mpo")
    core = lax.rem(n, 2)
    near, far = n + 1 - 2 * core, n - 1 + 2 * core
    beside = (lax.rem(x + 1, 4), lax.rem(x + 3, 4))
    inside = (far >= 0) & (far < rows)
    targets, steps = [entry(row, x) for row in TARGETS], (entry(STEP_UP, x), entry(STEP_DOWN, x))

    psi_load = pltpu.make_async_copy(psi.at[0], own_row, psi_sem)
    right_load = [pltpu.make_async_copy(right.at[:, 0, targets[k]], rights.at[k], right_sem.at[k]) for k in range(STEPS)]
    left_load = [
        [pltpu.make_async_copy(left.at[:, 0, targets[k], :, pl.ds(i * HALF, HALF)], lefts.at[k, i], left_sem.at[k, i]) for i in range(2)]
        for k in range(STEPS)
    ]

    def remote(src, dst, send, recv, device):
        return pltpu.make_async_remote_copy(src_ref=src, dst_ref=dst, send_sem=send, recv_sem=recv, device_id=device, device_id_type=MESH)

    def far_copy(k, i):
        if k == 0:
            span = rows_at(x * QUARTER + i * EIGHTH, EIGHTH)
        elif k == 1:
            span = rows_at(lax.rem(x + 2 * i, 4) * QUARTER, QUARTER)
        else:
            span = pl.ds(i * HALF, HALF)
        return remote(psi.at[0, SECTORS[k], span], far_row.at[SECTORS[k], span], far_send.at[k, i], far_recv.at[k, i], (far, x))

    def near_copy(k):
        return remote(psi.at[0, SECTORS[k]], near_row.at[SECTORS[k]], near_send.at[k], near_recv.at[k], (near, x))

    def hop1(side, piece, owner):
        there = far_row.at[SECTORS[0], rows_at(owner * QUARTER + (piece ^ side) * EIGHTH, EIGHTH)]
        return remote(there, there, hop1_send.at[side, piece], hop1_recv.at[side, piece], (n, beside[side]))

    def hop2(side, owner):
        there = far_row.at[SECTORS[0], rows_at(owner * QUARTER + side * EIGHTH, EIGHTH)]
        return remote(there, there, hop2_send.at[side], hop2_recv.at[side], (n, beside[side]))

    def share(side, owner):
        there = far_row.at[SECTORS[1], rows_at(owner * QUARTER, QUARTER)]
        return remote(there, there, share_send.at[side], share_recv.at[side], (n, beside[side]))

    def mid_copy(k, side, c):
        there = sends.at[k, pl.ds(side * HALF + c * QUARTER, QUARTER)]
        return remote(there, middle.at[side, pl.ds(c * QUARTER, QUARTER)], mid_send.at[side, c], mid_recv.at[side, c], (n, beside[side]))

    def whole_copy(k, side, c):
        span = pl.ds((1 - side) * HALF + c * QUARTER, QUARTER)
        return remote(sends.at[k, span], parts.at[side, span], whole_send.at[side, c], whole_recv.at[side, c], (n, beside[side]))

    def added_copy(side, c):
        span = pl.ds(side * HALF + c * QUARTER, QUARTER)
        return remote(sends.at[steps[side], span], parts.at[side, span], added_send.at[side, c], added_recv.at[side, c], (n, beside[side]))

    barrier = pltpu.get_barrier_semaphore()
    for device in ((near, x), (n, beside[0]), (n, beside[1])):
        pl.semaphore_signal(barrier, inc=1, device_id=device, device_id_type=MESH)

    @pl.when(inside)
    def _():
        pl.semaphore_signal(barrier, inc=1, device_id=(far, x), device_id_type=MESH)

    psi_load.start()
    for k in range(STEPS):
        right_load[k].start()
        left_load[k][0].start()
        left_load[k][1].start()

    pl.semaphore_wait(barrier, 3 + ((n + rows - 1) // rows) * ((2 * rows - 2 - n) // rows))

    @pl.when(inside)
    def _():
        for k, i in ((0, 0), (0, 1), (1, 0), (2, 0), (2, 1), (1, 1), (3, 0), (3, 1)):
            far_copy(k, i).start()

    for k in (0, 2, 1, 3):
        near_copy(k).start()

    @pl.when(inside)
    def _():
        for side in range(2):
            far_copy(0, side).wait_recv()
            hop1(side, 0, x).start()
        for side in range(2):
            hop1(side, 1, x).start()
        for side in range(2):
            hop1(side, 0, beside[1 - side]).wait_recv()
            hop2(side, beside[1 - side]).start()
        far_copy(1, 0).wait_recv()
        for side in range(2):
            share(side, x).start()

    def source(w, t, span):
        first, last = (3 - t) // 3, t // 3
        low, high = t - 1 + 2 * first, t + 1 - 2 * last
        row, col = shifts[0, w], shifts[1, w]
        outside = ((row > 0) & (n == 0)) | ((row < 0) & (n == rows - 1)) | ((col > 0) & (t == 0)) | ((col < 0) & (t == 3))
        from_far = (row > 0) == (core == 0)
        away = jnp.where(from_far, jnp.where(col > 0, far_row[low, span], far_row[high, span]),
                         jnp.where(col > 0, near_row[low, span], near_row[high, span]))
        block = jnp.where(row == 0, own_row[t, span], away)
        return jnp.where(outside, jnp.zeros_like(block), block)

    def products(k, span):
        return [dot(source(w, targets[k], span), rights[k, w]).astype(bf16) for w in range(TERMS)]

    def order(k):
        up = (targets[k] == beside[0]).astype(jnp.int32) if k < 3 else 0
        return (up, 1 - up)

    def keep(k, span, total):
        sums[k, span] = total
        if k < 3:
            sends[k, span] = total.astype(bf16)

    def send(k, r, c):
        pl.when(targets[k] == lax.rem(x + 2, 4))(mid_copy(k, r, c).start)
        if r == 0:
            for side in range(2):
                pl.when(targets[k] == beside[side])(whole_copy(k, side, c).start)

    def first_half(k):
        right_load[k].wait()
        left_load[k][0].wait()
        inner = products(k, pl.ds(0, HALF))
        sums[k] = sum(dot(lefts[k, 0, w], inner[w]) for w in range(TERMS))

    def finish(k, total):
        for r, half in enumerate(order(k)):
            if r == 0 and k < 3:
                for c in range(2):
                    span = rows_at(half * HALF + c * QUARTER, QUARTER)
                    keep(k, span, total(span))
                    send(k, r, c)
            else:
                span = rows_at(half * HALF, HALF)
                keep(k, span, total(span))
                if k < 3:
                    for c in range(2):
                        send(k, r, c)

    def second_half(k):
        left_load[k][1].wait()
        inner = products(k, pl.ds(HALF, HALF))
        finish(k, lambda span: sums[k, span] + sum(dot(lefts[k, 1, w, span], inner[w]) for w in range(TERMS)))

    def at_once(k):
        right_load[k].wait()
        left_load[k][0].wait()
        left_load[k][1].wait()
        inner = products(k, pl.ds(0, 2 * HALF))
        finish(k, lambda span: sum(dot(lefts[k, i, w, span], inner[w][i * HALF:(i + 1) * HALF]) for w in range(TERMS) for i in range(2)))

    def arrived(k, i, where):
        pl.when(inside & where)(far_copy(k, i).wait_recv)

    psi_load.wait()
    for k in range(STEPS):
        near_copy(k).wait_recv()

    @pl.when(inside)
    def _():
        for side in range(2):
            hop1(side, 1, beside[1 - side]).wait_recv()
            hop2(side, lax.rem(x + 2, 4)).wait_recv()

    arrived(2, 0, x == 3)
    arrived(2, 1, x == 3)
    at_once(0)

    arrived(1, 1, x >= 0)
    arrived(2, 0, x != 3)
    arrived(2, 1, x != 3)

    @pl.when(inside)
    def _():
        for side in range(2):
            share(side, beside[1 - side]).wait_recv()

    at_once(1)

    arrived(3, 0, x != 2)
    first_half(2)
    arrived(3, 1, x != 2)
    second_half(2)

    def add_on():
        for c in range(2):
            for side in range(2):
                if c == 0:
                    for i in range(2):
                        mid_copy(0, side, i).wait_send()
                mid_copy(0, side, c).wait_recv()
                span = pl.ds(side * HALF + c * QUARTER, QUARTER)
                sends[steps[side], span] = (sums[steps[side], span] + middle[side, pl.ds(c * QUARTER, QUARTER)].astype(f32)).astype(bf16)
                added_copy(side, c).start()

    even = lax.rem(x, 2) == 0
    pl.when(even)(add_on)
    arrived(3, 0, x == 2)
    arrived(3, 1, x == 2)
    at_once(3)

    pl.when(jnp.logical_not(even))(add_on)

    for side in range(2):
        for c in range(2):
            whole_copy(0, side, c).wait_recv()
    for c in range(2):
        for side in range(2):
            added_copy(side, c).wait_recv()
            span = pl.ds(side * HALF + c * QUARTER, QUARTER)
            out[0, 0, span] = (sums[3, span] + parts[0, span].astype(f32) + parts[1, span].astype(f32)).astype(bf16)

    for k in range(STEPS):
        near_copy(k).wait_send()
    for side in range(2):
        for c in range(2):
            whole_copy(0, side, c).wait_send()
            added_copy(side, c).wait_send()

    @pl.when(inside)
    def _():
        for k in range(STEPS):
            for i in range(2):
                far_copy(k, i).wait_send()
        for side in range(2):
            share(side, x).wait_send()
            hop2(side, x).wait_send()
            for piece in range(2):
                hop1(side, piece, x).wait_send()


def per_device(rows, psi, left_env, right_env, shifts):
    terms, _, sectors, width, _ = left_env.shape
    block = (width, width)
    pairs = pltpu.SemaphoreType.DMA((STEPS, 2))
    singles = pltpu.SemaphoreType.DMA((STEPS,))
    return pl.pallas_call(
        functools.partial(kernel, rows),
        out_shape=pltpu.VMEM((1, 1) + block, bf16),
        in_specs=[pl.BlockSpec(memory_space=pltpu.SMEM)] + [pl.BlockSpec(memory_space=pl.ANY)] * 3,
        out_specs=pl.BlockSpec(memory_space=pltpu.VMEM),
        scratch_shapes=[
            pltpu.VMEM((STEPS, 2, terms, width, HALF), bf16),
            pltpu.VMEM((STEPS, terms) + block, bf16),
            pltpu.VMEM((sectors,) + block, bf16),
            pltpu.VMEM((sectors,) + block, bf16),
            pltpu.VMEM((sectors,) + block, bf16),
            pltpu.VMEM((STEPS,) + block, f32),
            pltpu.VMEM((STEPS,) + block, bf16),
            pltpu.VMEM((2, HALF, width), bf16),
            pltpu.VMEM((2,) + block, bf16),
            pairs,
            singles,
            pltpu.SemaphoreType.DMA,
            pairs,
            pairs,
            singles,
            singles,
        ] + [pltpu.SemaphoreType.DMA((2, 2))] * 2 + [pltpu.SemaphoreType.DMA((2,))] * 4 + [pltpu.SemaphoreType.DMA((2, 2))] * 2 + [pltpu.SemaphoreType.DMA((2, 2))] * 2 + [pltpu.SemaphoreType.DMA((2, 2))] * 2,
        compiler_params=pltpu.CompilerParams(collective_id=0, has_side_effects=True, vmem_limit_bytes=56 << 20),
        cost_estimate=pl.CostEstimate(flops=4 * terms * sectors * width**3, bytes_accessed=36 << 20, transcendentals=0),
    )(shifts.T, psi, left_env, right_env)


def solution(mesh):
    return jax.shard_map(
        functools.partial(per_device, mesh.shape["sec"]),
        mesh=mesh,
        in_specs=(
            P("sec", None, None, None),
            P("mpo", "sec", None, None, None),
            P("mpo", "sec", None, None, None),
            P("mpo", None),
        ),
        out_specs=P("sec", "mpo", None, None),
        check_vma=False,
    )
```

```python
import functools

import jax
import jax.numpy as jnp
from jax import lax
from jax.experimental import pallas as pl
from jax.experimental.pallas import tpu as pltpu
from jax.sharding import PartitionSpec as P

MESH = pl.DeviceIdType.MESH
f32, bf16 = jnp.float32, jnp.bfloat16
dot = functools.partial(jnp.dot, preferred_element_type=f32)

SECTORS = (2, 1, 0, 3)
TARGETS = ((3, 3, 3, 1), (1, 0, 1, 0), (2, 2, 0, 2), (0, 1, 2, 3))
STEP_UP, STEP_DOWN = (1, 2, 0, 1), (0, 1, 1, 2)
STEPS, TERMS, HALF, QUARTER, EIGHTH = 4, 4, 256, 128, 64


def entry(row, x):
    code = sum(value * 4**i for i, value in enumerate(row))
    power = (1 + 3 * lax.rem(x, 2)) * (1 + 15 * (x // 2))
    return lax.rem(code // power, 4)


def rows_at(start, size):
    return pl.ds(pl.multiple_of(start, size), size)


def kernel(rows, shifts, psi, left, right, out, lefts, rights, own_row, far_row, near_row, sums, kept, sends, middle, parts,
           left_sem, right_sem, psi_sem, far_send, far_recv, near_send, near_recv, hop1_send, hop1_recv, hop2_send, hop2_recv, share_send, share_recv,
           mid_send, mid_recv, whole_send, whole_recv, added_send, added_recv):
    n, x = lax.axis_index("sec"), lax.axis_index("mpo")
    core = lax.rem(n, 2)
    near, far = n + 1 - 2 * core, n - 1 + 2 * core
    beside = (lax.rem(x + 1, 4), lax.rem(x + 3, 4))
    inside = (far >= 0) & (far < rows)
    targets, steps = [entry(row, x) for row in TARGETS], (entry(STEP_UP, x), entry(STEP_DOWN, x))

    psi_load = pltpu.make_async_copy(psi.at[0], own_row, psi_sem)
    right_load = [pltpu.make_async_copy(right.at[:, 0, targets[k]], rights.at[k], right_sem.at[k]) for k in range(STEPS)]
    left_load = [
        [pltpu.make_async_copy(left.at[:, 0, targets[k], :, pl.ds(i * HALF, HALF)], lefts.at[k, i], left_sem.at[k, i]) for i in range(2)]
        for k in range(STEPS)
    ]

    def remote(src, dst, send, recv, device):
        return pltpu.make_async_remote_copy(src_ref=src, dst_ref=dst, send_sem=send, recv_sem=recv, device_id=device, device_id_type=MESH)

    def far_copy(k, i):
        if k == 0:
            span = rows_at(x * QUARTER + i * EIGHTH, EIGHTH)
        elif k == 1:
            span = rows_at(lax.rem(x + 2 * i, 4) * QUARTER, QUARTER)
        else:
            span = pl.ds(i * HALF, HALF)
        return remote(psi.at[0, SECTORS[k], span], far_row.at[SECTORS[k], span], far_send.at[k, i], far_recv.at[k, i], (far, x))

    def near_copy(k):
        return remote(psi.at[0, SECTORS[k]], near_row.at[SECTORS[k]], near_send.at[k], near_recv.at[k], (near, x))

    def hop1(side, piece, owner):
        there = far_row.at[SECTORS[0], rows_at(owner * QUARTER + (piece ^ side) * EIGHTH, EIGHTH)]
        return remote(there, there, hop1_send.at[side, piece], hop1_recv.at[side, piece], (n, beside[side]))

    def hop2(side, owner):
        there = far_row.at[SECTORS[0], rows_at(owner * QUARTER + side * EIGHTH, EIGHTH)]
        return remote(there, there, hop2_send.at[side], hop2_recv.at[side], (n, beside[side]))

    def share(side, owner):
        there = far_row.at[SECTORS[1], rows_at(owner * QUARTER, QUARTER)]
        return remote(there, there, share_send.at[side], share_recv.at[side], (n, beside[side]))

    def mid_copy(k, side, c):
        there = sends.at[k, pl.ds(side * HALF + c * QUARTER, QUARTER)]
        return remote(there, middle.at[side, pl.ds(c * QUARTER, QUARTER)], mid_send.at[side, c], mid_recv.at[side, c], (n, beside[side]))

    def whole_copy(k, side, c):
        span = pl.ds((1 - side) * HALF + c * QUARTER, QUARTER)
        return remote(sends.at[k, span], parts.at[side, span], whole_send.at[side, c], whole_recv.at[side, c], (n, beside[side]))

    def added_copy(side, c):
        span = pl.ds(side * HALF + c * QUARTER, QUARTER)
        return remote(sends.at[steps[side], span], parts.at[side, span], added_send.at[side, c], added_recv.at[side, c], (n, beside[side]))

    barrier = pltpu.get_barrier_semaphore()
    for device in ((near, x), (n, beside[0]), (n, beside[1])):
        pl.semaphore_signal(barrier, inc=1, device_id=device, device_id_type=MESH)

    @pl.when(inside)
    def _():
        pl.semaphore_signal(barrier, inc=1, device_id=(far, x), device_id_type=MESH)

    psi_load.start()
    for k in range(STEPS):
        right_load[k].start()
        left_load[k][0].start()
        left_load[k][1].start()

    pl.semaphore_wait(barrier, 3 + ((n + rows - 1) // rows) * ((2 * rows - 2 - n) // rows))

    @pl.when(inside)
    def _():
        for k, i in ((0, 0), (0, 1), (1, 0), (2, 0), (2, 1), (1, 1), (3, 0), (3, 1)):
            far_copy(k, i).start()

    for k in (0, 2, 1, 3):
        near_copy(k).start()

    @pl.when(inside)
    def _():
        for side in range(2):
            far_copy(0, side).wait_recv()
            hop1(side, 0, x).start()
        for side in range(2):
            hop1(side, 1, x).start()
        for side in range(2):
            hop1(side, 0, beside[1 - side]).wait_recv()
            hop2(side, beside[1 - side]).start()
        far_copy(1, 0).wait_recv()
        for side in range(2):
            share(side, x).start()

    def source(w, t, span):
        first, last = (3 - t) // 3, t // 3
        low, high = t - 1 + 2 * first, t + 1 - 2 * last
        row, col = shifts[0, w], shifts[1, w]
        outside = ((row > 0) & (n == 0)) | ((row < 0) & (n == rows - 1)) | ((col > 0) & (t == 0)) | ((col < 0) & (t == 3))
        from_far = (row > 0) == (core == 0)
        away = jnp.where(from_far, jnp.where(col > 0, far_row[low, span], far_row[high, span]),
                         jnp.where(col > 0, near_row[low, span], near_row[high, span]))
        block = jnp.where(row == 0, own_row[t, span], away)
        return jnp.where(outside, jnp.zeros_like(block), block)

    def products(k, span):
        return [dot(source(w, targets[k], span), rights[k, w]).astype(bf16) for w in range(TERMS)]

    def order(k):
        up = (targets[k] == beside[0]).astype(jnp.int32) if k < 3 else 0
        return (up, 1 - up)

    def keep(k, span, total):
        sums[k, span] = total
        if k < 3:
            sends[k, span] = total.astype(bf16)

    def send(k, r, c):
        pl.when(targets[k] == lax.rem(x + 2, 4))(mid_copy(k, r, c).start)
        if r == 0:
            for side in range(2):
                pl.when(targets[k] == beside[side])(whole_copy(k, side, c).start)

    def first_half(k):
        right_load[k].wait()
        left_load[k][0].wait()
        inner = products(k, pl.ds(0, HALF))
        sums[k] = sum(dot(lefts[k, 0, w], inner[w]) for w in range(TERMS))

    def finish(k, total):
        for r, half in enumerate(order(k)):
            if r == 0 and k < 3:
                for c in range(2):
                    span = rows_at(half * HALF + c * QUARTER, QUARTER)
                    keep(k, span, total(span))
                    send(k, r, c)
            elif k > 0:
                span = rows_at(half * HALF, HALF)
                keep(k, span, total(span))
                if k < 3:
                    for c in range(2):
                        send(k, r, c)

    def second_half(k):
        left_load[k][1].wait()
        inner = products(k, pl.ds(HALF, HALF))
        finish(k, lambda span: sums[k, span] + sum(dot(lefts[k, 1, w, span], inner[w]) for w in range(TERMS)))

    def at_once(k):
        right_load[k].wait()
        left_load[k][0].wait()
        left_load[k][1].wait()
        inner = products(k, pl.ds(0, 2 * HALF))
        if k == 0:
            for w in range(TERMS):
                kept[w] = inner[w]
        finish(k, lambda span: sum(dot(lefts[k, i, w, span], inner[w][i * HALF:(i + 1) * HALF]) for w in range(TERMS) for i in range(2)))

    def rest():
        span = rows_at(order(0)[1] * HALF, HALF)
        keep(0, span, sum(dot(lefts[0, i, w, span], kept[w, pl.ds(i * HALF, HALF)]) for w in range(TERMS) for i in range(2)))
        for c in range(2):
            send(0, 1, c)

    def arrived(k, i, where):
        pl.when(inside & where)(far_copy(k, i).wait_recv)

    psi_load.wait()
    for k in range(STEPS):
        near_copy(k).wait_recv()

    @pl.when(inside)
    def _():
        for side in range(2):
            hop1(side, 1, beside[1 - side]).wait_recv()
            hop2(side, lax.rem(x + 2, 4)).wait_recv()

    arrived(2, 0, x == 3)
    arrived(2, 1, x == 3)
    even = lax.rem(x, 2) == 0
    at_once(0)
    pl.when(jnp.logical_not(even))(rest)

    arrived(1, 1, x >= 0)
    arrived(2, 0, x != 3)
    arrived(2, 1, x != 3)

    @pl.when(inside)
    def _():
        for side in range(2):
            share(side, beside[1 - side]).wait_recv()

    at_once(1)
    pl.when(even)(rest)

    arrived(3, 0, x != 2)
    first_half(2)
    arrived(3, 1, x != 2)
    second_half(2)

    def add_on():
        for c in range(2):
            for side in range(2):
                if c == 0:
                    for i in range(2):
                        mid_copy(0, side, i).wait_send()
                mid_copy(0, side, c).wait_recv()
                span = pl.ds(side * HALF + c * QUARTER, QUARTER)
                sends[steps[side], span] = (sums[steps[side], span] + middle[side, pl.ds(c * QUARTER, QUARTER)].astype(f32)).astype(bf16)
                added_copy(side, c).start()

    pl.when(even)(add_on)
    arrived(3, 0, x == 2)
    arrived(3, 1, x == 2)
    at_once(3)

    pl.when(jnp.logical_not(even))(add_on)

    for side in range(2):
        for c in range(2):
            whole_copy(0, side, c).wait_recv()
    for c in range(2):
        for side in range(2):
            added_copy(side, c).wait_recv()
            span = pl.ds(side * HALF + c * QUARTER, QUARTER)
            out[0, 0, span] = (sums[3, span] + parts[0, span].astype(f32) + parts[1, span].astype(f32)).astype(bf16)

    for k in range(STEPS):
        near_copy(k).wait_send()
    for side in range(2):
        for c in range(2):
            whole_copy(0, side, c).wait_send()
            added_copy(side, c).wait_send()

    @pl.when(inside)
    def _():
        for k in range(STEPS):
            for i in range(2):
                far_copy(k, i).wait_send()
        for side in range(2):
            share(side, x).wait_send()
            hop2(side, x).wait_send()
            for piece in range(2):
                hop1(side, piece, x).wait_send()


def per_device(rows, psi, left_env, right_env, shifts):
    terms, _, sectors, width, _ = left_env.shape
    block = (width, width)
    pairs = pltpu.SemaphoreType.DMA((STEPS, 2))
    singles = pltpu.SemaphoreType.DMA((STEPS,))
    return pl.pallas_call(
        functools.partial(kernel, rows),
        out_shape=pltpu.VMEM((1, 1) + block, bf16),
        in_specs=[pl.BlockSpec(memory_space=pltpu.SMEM)] + [pl.BlockSpec(memory_space=pl.ANY)] * 3,
        out_specs=pl.BlockSpec(memory_space=pltpu.VMEM),
        scratch_shapes=[
            pltpu.VMEM((STEPS, 2, terms, width, HALF), bf16),
            pltpu.VMEM((STEPS, terms) + block, bf16),
            pltpu.VMEM((sectors,) + block, bf16),
            pltpu.VMEM((sectors,) + block, bf16),
            pltpu.VMEM((sectors,) + block, bf16),
            pltpu.VMEM((STEPS,) + block, f32),
            pltpu.VMEM((TERMS,) + block, bf16),
            pltpu.VMEM((STEPS,) + block, bf16),
            pltpu.VMEM((2, HALF, width), bf16),
            pltpu.VMEM((2,) + block, bf16),
            pairs,
            singles,
            pltpu.SemaphoreType.DMA,
            pairs,
            pairs,
            singles,
            singles,
        ] + [pltpu.SemaphoreType.DMA((2, 2))] * 2 + [pltpu.SemaphoreType.DMA((2,))] * 4 + [pltpu.SemaphoreType.DMA((2, 2))] * 2 + [pltpu.SemaphoreType.DMA((2, 2))] * 2 + [pltpu.SemaphoreType.DMA((2, 2))] * 2,
        compiler_params=pltpu.CompilerParams(collective_id=0, has_side_effects=True, vmem_limit_bytes=56 << 20),
        cost_estimate=pl.CostEstimate(flops=4 * terms * sectors * width**3, bytes_accessed=36 << 20, transcendentals=0),
    )(shifts.T, psi, left_env, right_env)


def solution(mesh):
    return jax.shard_map(
        functools.partial(per_device, mesh.shape["sec"]),
        mesh=mesh,
        in_specs=(
            P("sec", None, None, None),
            P("mpo", "sec", None, None, None),
            P("mpo", "sec", None, None, None),
            P("mpo", None),
        ),
        out_specs=P("sec", "mpo", None, None),
        check_vma=False,
    )
```
